256 devices in a mesh: row: 32 (over z, y), col: 4 (over x_hi, core), depth: 2 (over x_lo).
Axes of the slice: x: 4 (x_hi: 2, x_lo: 2; x = x_hi * 2 + x_lo), y: 4, z: 8, core: 2. Of those that a mesh axis runs over, the one named last changes fastest.
Arguments:
- src_emb: bfloat16 [2, 512, 32768], P('depth', 'col', 'row'), may hold values from -6 to 6
- tgt_emb: bfloat16 [2, 512, 8192], P('depth', 'row', 'col'), may hold values from -6 to 6
- tile_mask: int32 [64, 16], P('row', 'col'), may hold values from 0 to 1, as said below
- src_mass: float32 [32768], P(('row', 'depth')), may hold values from 0.5 to 2
- tgt_mass: float32 [8192], P('col'), may hold values from 0.5 to 2
Outputs:
- log_src: float32 [32768], P(('row', 'depth'))
- log_tgt: float32 [8192], P('col')
The draws below stay inside these ranges and needn't reach their ends.
Inputs may be any that keep to these rules, and one draw needn't show every extreme that they name: `tile_mask`: every tile row and every tile column of the mask holds at least one 1.
All inputs are finite; a program needn't handle non-finite values.
Results may differ from the reference program's by a relative error of at most 0.0003.
Values may be sent and summed in bfloat16 or wider, within the bound.
No kernel may reach another device: no remote copies, remote signals or barrier semaphores. Data moves between devices by JAX's collectives and lax.ppermute only.
A program may use at most 64 MiB of HBM per device.

```python
import math
import jax
import jax.numpy as jnp
from jax import lax

VECTOR_DIMENSION = 1024
TILE = 512
ITERS = 3
NS = 32768
NT = 8192
MASK_ROWS = 64
MASK_COLS = 16
N_DEPTH = 2


def draw_tile_mask(key, part):
    key = jax.random.fold_in(key, 7)
    random_key_level, key_roll, key_shift = jax.random.split(key, 3)
    level = jax.random.randint(random_key_level, (MASK_ROWS, 1), 0, 5)
    roll = jax.random.randint(key_roll, (MASK_ROWS, MASK_COLS), 0, 8)
    offset = jax.random.randint(key_shift, (), 0, MASK_COLS)
    tile_rows = jnp.arange(MASK_ROWS, dtype=jnp.int32)[:, None]
    tile_cols = jnp.arange(MASK_COLS, dtype=jnp.int32)[None, :]
    forced_entries = tile_cols == (tile_rows + offset) % MASK_COLS
    return jnp.where(forced_entries | (roll < level), 1, 0).astype(jnp.int32)


def level_of(key, dims, shards, least, top_value):
    def one(position, shards_of):
        steps = jax.random.uniform(jax.random.fold_in(jax.random.fold_in(key, 6), position), (shards_of,), jnp.float32, least / len(shards), top_value / len(shards))
        return jnp.repeat(jnp.exp(steps), dims[position] // shards_of).reshape((-1,) + (1,) * (len(dims) - position - 1))

    level = one(*shards[0])
    for cut in shards[1:]:
        level = level * one(*cut)
    return level


def noise(key, shape, scale, limit, cuts=(), held_as=jnp.bfloat16):
    loudness = level_of(key, shape, cuts, -0.22, 0.18) if cuts else 1.0
    result = jax.random.normal(key, shape, jnp.float32) * scale * loudness
    return jnp.minimum(jnp.maximum(result, -limit), limit).astype(held_as)


def setup_inputs(seed: int = 0) -> dict:
    arg_keys = jax.random.split(jax.random.key(seed), 6)
    src_emb = noise(arg_keys[0], (N_DEPTH, VECTOR_DIMENSION // N_DEPTH, NS), 1.0, 6.0, ((0, 2), (1, 4), (2, 32)))
    tgt_emb = noise(arg_keys[1], (N_DEPTH, VECTOR_DIMENSION // N_DEPTH, NT), 1.0, 6.0, ((0, 2), (1, 32), (2, 4)))
    tile_mask = draw_tile_mask(jax.random.fold_in(arg_keys[5], 71), 0)
    src_mass = jnp.clip(jnp.exp(math.log(2.0) - 1.3862944 * jax.random.uniform(arg_keys[3], (NS,), jnp.float32) ** level_of(arg_keys[3], (NS,), ((0, 64),), -0.2, 0.2)), 0.5, 2.0)
    tgt_mass = jnp.clip(jnp.exp(math.log(2.0) - 1.3862944 * jax.random.uniform(arg_keys[4], (NT,), jnp.float32) ** level_of(arg_keys[4], (NT,), ((0, 4),), -0.2, 0.2)), 0.5, 2.0)
    return dict(src_emb=src_emb, tgt_emb=tgt_emb, tile_mask=tile_mask, src_mass=src_mass, tgt_mass=tgt_mass)


smoothing_strength = 0.64

def reference(src_emb, tgt_emb, tile_mask, src_mass, tgt_mass):
    src_matrix = src_emb.reshape(VECTOR_DIMENSION, NS)
    destination_vectors = tgt_emb.reshape(VECTOR_DIMENSION, NT)
    sharpness_factor = 1.0 / (smoothing_strength * math.sqrt(VECTOR_DIMENSION))
    block_count = NS // TILE
    src_blocks = src_matrix.reshape(VECTOR_DIMENSION, block_count, TILE).transpose(1, 0, 2)

    def one_block(inputs):
        first_operand_block, row_of_mask = inputs
        similarity_matrix = lax.dot_general(first_operand_block, destination_vectors, (((0,), (0,)), ((), ())), preferred_element_type=jnp.float32) * sharpness_factor
        mask_wide = jnp.repeat(row_of_mask, TILE)[None, :]
        return jnp.where(mask_wide > 0, jnp.exp(similarity_matrix), jnp.float32(0.0))
    kernel = lax.map(one_block, (src_blocks, tile_mask)).reshape(NS, NT)
    tgt_scale = jnp.ones((NT,), jnp.float32)
    src_scale = jnp.ones((NS,), jnp.float32)
    for sweep_index in range(ITERS):
        src_scale = src_mass / jnp.dot(kernel, tgt_scale, precision=lax.Precision.HIGHEST)
        tgt_scale = tgt_mass / jnp.dot(src_scale, kernel, precision=lax.Precision.HIGHEST)
    return (jnp.log(src_scale), jnp.log(tgt_scale))
```

```python
import math

import jax
import jax.numpy as jnp
from jax import lax
from jax.experimental import pallas as pl
from jax.experimental.pallas import tpu as pltpu
from jax.sharding import Mesh
from jax.sharding import PartitionSpec as P

VECTOR_DIMENSION = 1024
TILE = 512
ITERS = 3
SHARPNESS = 1.0 / (0.64 * math.sqrt(VECTOR_DIMENSION))

X = ("xh", "xl")
PLANE = ("z", "y")
N_Z, N_Y, N_X = 8, 4, 4
ROWS = 1024
COLS = 1024
LANES = 128
CHUNKS = ROWS // LANES
GROUP = 16
F32 = jnp.float32
VMEM = pl.BlockSpec(memory_space=pltpu.VMEM)
SMEM = pl.BlockSpec(memory_space=pltpu.SMEM)


def shift(value, axis, size, by):
    return lax.ppermute(value, axis, [(i, (i + by) % size) for i in range(size)])


def lane_sums(folded):
    parts = [
        jnp.sum(folded[i * LANES : (i + 1) * LANES, :].T, axis=0, keepdims=True)
        for i in range(folded.shape[0] // LANES)
    ]
    return jnp.concatenate(parts, axis=0)


def build_body(where_ref, mask_ref, src_a_ref, src_b_ref, *refs):
    block_refs, (kernel_ref, sums_ref, tgt_ref, folded_ref) = refs[:-4], refs[-4:]
    z, y, c, xl = where_ref[0], where_ref[1], where_ref[2], where_ref[3]
    steps = (0, -1, 1, -2, 2, -3, 3, 4, 4)
    turns = (0, -1, 1, 2)
    for index, (block, step) in enumerate(zip(block_refs, steps, strict=True)):
        places = range(4) if index < 7 else (range(2) if index == 7 else range(2, 4))
        for row, place in enumerate(places):
            at = lax.rem(z + step + N_Z, N_Z) * N_Y + lax.rem(y + turns[place] + N_Y, N_Y)
            high, core, rest = lax.div(at, 16), lax.rem(lax.div(at, 8), 2), lax.rem(at, 8)
            side = jnp.where(core == c, 0, 1)
            for group in range(2):
                low = xl if group == 0 else 1 - xl
                to = side * 512 + (high * 2 + low) * 128 + rest * GROUP
                start = (row * 2 + group) * GROUP
                tgt_ref[pl.ds(pl.multiple_of(to, GROUP), GROUP), :] = block[start : start + GROUP, :]
    contract = (((0,), (0,)), ((), ()))
    for i in range(ROWS // TILE):
        rows = slice(i * TILE, (i + 1) * TILE)
        folded_ref[rows, :] = jnp.zeros((TILE, LANES), F32)
        for j in range(COLS // TILE):
            cols = slice(j * TILE, (j + 1) * TILE)
            live = mask_ref[i, j] > 0

            @pl.when(live)
            def _():
                scores = lax.dot_general(
                    src_a_ref[:, rows], tgt_ref[:512, cols], contract, preferred_element_type=F32
                ) + lax.dot_general(
                    src_b_ref[:, rows], tgt_ref[512:, cols], contract, preferred_element_type=F32
                )
                part = jnp.exp(scores * SHARPNESS)
                kernel_ref[rows, cols] = part
                total = part[:, :LANES]
                for k in range(1, TILE // LANES):
                    total = total + part[:, k * LANES : (k + 1) * LANES]
                folded_ref[rows, :] += total

            @pl.when(jnp.logical_not(live))
            def _():
                kernel_ref[rows, cols] = jnp.zeros((TILE, TILE), F32)

    sums_ref[...] = lane_sums(folded_ref[...])


def columns_body(kernel_ref, mass_ref, *refs):
    part_refs, (scale_ref, out_ref) = refs[:-2], refs[-2:]
    total = part_refs[0][...]
    for part in part_refs[1:]:
        total = total + part[...]
    scale = mass_ref[...] / total
    scale_ref[...] = scale
    acc = [None] * (COLS // LANES)
    for i in range(CHUNKS):
        wide = jnp.broadcast_to(scale[i : i + 1, :], (LANES, LANES)).T
        for j in range(COLS // LANES):
            prod = kernel_ref[i * LANES : (i + 1) * LANES, j * LANES : (j + 1) * LANES] * wide
            prod = jnp.sum(prod.reshape(LANES // 8, 8, LANES), axis=0)
            acc[j] = prod if acc[j] is None else acc[j] + prod
    sums = jnp.concatenate([jnp.sum(a, axis=0, keepdims=True) for a in acc], axis=0)
    out_ref[...] = jnp.broadcast_to(sums[None], out_ref.shape)


def rows_body(kernel_ref, mass_ref, parts_ref, sums_ref, folded_ref):
    scale = mass_ref[...] / jnp.sum(parts_ref[...], axis=0)
    for i in range(CHUNKS):
        rows = slice(i * LANES, (i + 1) * LANES)
        total = kernel_ref[rows, :LANES] * scale[0:1, :]
        for j in range(1, COLS // LANES):
            total = total + kernel_ref[rows, j * LANES : (j + 1) * LANES] * scale[j : j + 1, :]
        folded_ref[rows, :] = total
    sums_ref[...] = lane_sums(folded_ref[...])


SMALL = jax.ShapeDtypeStruct((CHUNKS, LANES), F32)
WIDE = jax.ShapeDtypeStruct((N_Z * N_Y, CHUNKS, LANES), F32)
KERNEL = jax.ShapeDtypeStruct((ROWS, COLS), F32)
PARAMS = pltpu.CompilerParams(vmem_limit_bytes=40 * 1024 * 1024)


def row_total(sums):
    chip = sums + shift(sums, "c", 2, 1)
    return (
        chip,
        shift(chip, X, N_X, 2),
        shift(chip, X, N_X, 1),
        shift(chip, X, N_X, -1),
    )


def shards(src_emb, tgt_emb, tile_mask, src_mass, tgt_mass):
    z, y, c, xl = (lax.axis_index(a) for a in ("z", "y", "c", "xl"))
    src_a = lax.all_gather(src_emb[0], X, axis=0, tiled=True)
    src_b = shift(src_a, "c", 2, 1)
    tgt = tgt_emb[0]
    kept = lax.dynamic_slice_in_dim(tgt, xl * COLS, COLS, 1)
    sent = lax.dynamic_slice_in_dim(tgt, (1 - xl) * COLS, COLS, 1)
    pair = jnp.concatenate([kept, shift(sent, "xl", 2, 1)], axis=0)
    plane = jnp.concatenate(
        [pair, shift(pair, "y", N_Y, 1), shift(pair, "y", N_Y, -1), shift(pair, "y", N_Y, 2)], axis=0
    )
    blocks = [plane]
    up = down = plane
    for _ in range(3):
        up, down = shift(up, "z", N_Z, 1), shift(down, "z", N_Z, -1)
        blocks += [up, down]
    half = plane.shape[0] // 2
    blocks += [shift(up[:half], "z", N_Z, 1), shift(down[half:], "z", N_Z, -1)]

    other = shift(src_mass, "xl", 2, 1)
    src_rows = jnp.where(
        xl == 0, jnp.concatenate([src_mass, other]), jnp.concatenate([other, src_mass])
    ).reshape(CHUNKS, LANES)
    tgt_cols = lax.dynamic_slice_in_dim(tgt_mass, xl * COLS, COLS, 0).reshape(CHUNKS, LANES)
    mask = lax.dynamic_slice_in_dim(tile_mask, xl * (COLS // TILE), COLS // TILE, 1)
    where = jnp.stack([z, y, c, xl]).astype(jnp.int32)

    kernel, sums = pl.pallas_call(
        build_body,
        out_shape=(KERNEL, SMALL),
        in_specs=[SMEM, SMEM] + [VMEM] * (2 + len(blocks)),
        out_specs=(VMEM, VMEM),
        scratch_shapes=[
            pltpu.VMEM((VECTOR_DIMENSION, COLS), jnp.bfloat16),
            pltpu.VMEM((ROWS, LANES), F32),
        ],
        compiler_params=PARAMS,
    )(where, mask, src_a, src_b, *blocks)

    for sweep in range(ITERS):
        src_scale, sent = pl.pallas_call(
            columns_body,
            out_shape=(SMALL, WIDE),
            in_specs=[VMEM] * 6,
            out_specs=(VMEM, VMEM),
            compiler_params=PARAMS,
        )(kernel, src_rows, *row_total(sums))
        parts = lax.all_to_all(sent, PLANE, 0, 0, tiled=True)
        if sweep < ITERS - 1:
            sums = pl.pallas_call(
                rows_body,
                out_shape=SMALL,
                in_specs=[VMEM] * 3,
                out_specs=VMEM,
                scratch_shapes=[pltpu.VMEM((ROWS, LANES), F32)],
                compiler_params=PARAMS,
            )(kernel, tgt_cols, parts)

    log_src = jnp.log(lax.dynamic_slice_in_dim(src_scale, xl * (CHUNKS // 2), CHUNKS // 2, 0)).reshape(-1)
    mine = jnp.log(tgt_cols / jnp.sum(parts, axis=0)).reshape(-1)
    other = shift(mine, "xl", 2, 1)
    log_tgt = jnp.where(xl == 0, jnp.concatenate([mine, other]), jnp.concatenate([other, mine]))
    return log_src, log_tgt


def solution(mesh):
    fine = Mesh(mesh.devices.reshape(N_Z, N_Y, 2, 2, 2), ("z", "y", "xh", "c", "xl"))
    placed = (
        P("xl", ("xh", "c"), ("z", "y")),
        P("xl", ("z", "y"), ("xh", "c")),
        P(("z", "y"), ("xh", "c")),
        P(("z", "y", "xl")),
        P(("xh", "c")),
    )
    return jax.shard_map(
        shards,
        mesh=fine,
        in_specs=placed,
        out_specs=(P(("z", "y", "xl")), P(("xh", "c"))),
        check_vma=False,
    )
```

```python
import math

import jax
import jax.numpy as jnp
from jax import lax
from jax.experimental import pallas as pl
from jax.experimental.pallas import tpu as pltpu
from jax.sharding import Mesh
from jax.sharding import PartitionSpec as P

VECTOR_DIMENSION = 1024
TILE = 512
ITERS = 3
SHARPNESS = 1.0 / (0.64 * math.sqrt(VECTOR_DIMENSION))

X = ("xh", "xl")
PLANE = ("z", "y")
N_Z, N_Y, N_X = 8, 4, 4
ROWS = 1024
COLS = 1024
LANES = 128
CHUNKS = ROWS // LANES
GROUP = 16
F32 = jnp.float32
VMEM = pl.BlockSpec(memory_space=pltpu.VMEM)
HBM = pl.BlockSpec(memory_space=pltpu.HBM)
SMEM = pl.BlockSpec(memory_space=pltpu.SMEM)


def shift(value, axis, size, by):
    return lax.ppermute(value, axis, [(i, (i + by) % size) for i in range(size)])


def wheel(value, by):
    pairs = [
        (i * 2 + c, (i + (by if c == 0 else -by)) % N_Z * 2 + c) for i in range(N_Z) for c in range(2)
    ]
    return lax.ppermute(value, ("z", "c"), pairs)


def wheel_x(value, by):
    place = lambda x, c: x // 2 * 4 + c * 2 + x % 2
    pairs = [
        (place(i, c), place((i + (by if c == 0 else -by)) % N_X, c)) for i in range(N_X) for c in range(2)
    ]
    return lax.ppermute(value, ("xh", "c", "xl"), pairs)


def in_vmem(value):
    return pltpu.with_memory_space_constraint(value, pltpu.VMEM)


def in_hbm(value):
    return pltpu.with_memory_space_constraint(value, pltpu.HBM)


def lane_sums(folded):
    parts = [
        jnp.sum(folded[i * LANES : (i + 1) * LANES, :].T, axis=0, keepdims=True)
        for i in range(folded.shape[0] // LANES)
    ]
    return jnp.concatenate(parts, axis=0)


def natural(low, z, y):
    return pl.multiple_of(low * 512 + z * (N_Y * GROUP) + y * GROUP, GROUP)


def turned(value, size):
    return lax.rem(value + size, size)


CONTRACT = (((0,), (0,)), ((), ()))
TURNS = (0, -1, 1, 2)
STEPS = (0, -1, 1, -2, 2, -3, 3)


def halves_body(tgt_ref, out_ref):
    for y in range(N_Y):
        for low in range(2):
            out_ref[y * 2 + low] = tgt_ref[:, low * COLS : (low + 1) * COLS]


def partial_body(where_ref, mask_hbm, tgt_mass_hbm, src_hbm, *refs):
    src_refs, block_refs = refs[:7], refs[7:14]
    scores_ref, src_last_ref, live_ref, tgt_cols_ref, side_ref = refs[14:19]
    src_ref, tgt_ref, mask_ref, tgt_mass_ref, sems = refs[19:]
    z, c, xh, xl = (where_ref[i] for i in range(4))

    def src_at(core, turn):
        x = turned(xh * 2 + xl + turn * (1 - 2 * core), N_X)
        to = lax.rem(x, 2) * 512 + lax.div(x, 2) * 256 + core * 128
        return src_ref.at[pl.ds(pl.multiple_of(to, LANES), LANES), :]

    fetches = [
        pltpu.make_async_copy(src_hbm, src_at(c, 0), sems.at[0]),
        pltpu.make_async_copy(mask_hbm, mask_ref, sems.at[1]),
        pltpu.make_async_copy(tgt_mass_hbm, tgt_mass_ref, sems.at[2]),
    ]
    for fetch in fetches:
        fetch.start()
    for index, part in enumerate(src_refs):
        core, turn = (c, index + 1) if index < 3 else (1 - c, index - 3)
        src_at(core, TURNS[turn])[...] = part[...]
    for block, step in zip(block_refs, STEPS, strict=True):
        plane = turned(z + step * (1 - 2 * c), N_Z)
        for place in range(4):
            for low in range(2):
                to = natural(low, plane, place)
                start = (place * 2 + low) * GROUP
                tgt_ref[pl.ds(to, GROUP), :] = block[start : start + GROUP, :]
    plane = turned(z + 4, N_Z)
    for low in range(2):
        tgt_ref[pl.ds(natural(low, plane, 0), N_Y * GROUP), :] = jnp.zeros((N_Y * GROUP, COLS), jnp.bfloat16)
    for fetch in fetches:
        fetch.wait()
    for place in range(4):
        for low in range(2):
            start = (place * 2 + low) * GROUP
            src_last_ref[start : start + GROUP, :] = src_ref[pl.ds(natural(low, plane, place), GROUP), :]
    tgt_cols_ref[...] = jnp.where(xl == 0, tgt_mass_ref[:CHUNKS, :], tgt_mass_ref[CHUNKS:, :])
    side_ref[...] = jnp.full(side_ref.shape, xl.astype(F32))
    for i in range(ROWS // TILE):
        rows = slice(i * TILE, (i + 1) * TILE)
        for j in range(COLS // TILE):
            cols = slice(j * TILE, (j + 1) * TILE)
            live = mask_ref[i, xl * (COLS // TILE) + j] > 0
            live_ref[i, j] = jnp.full((8, LANES), live.astype(F32))

            @pl.when(live)
            def _():
                scores_ref[rows, cols] = lax.dot_general(
                    src_ref[:, rows], tgt_ref[:, cols], CONTRACT, preferred_element_type=F32
                )


def build_body(src_last_ref, scores_ref, live_ref, mass_ref, block_ref, kernel_ref, sums_ref, folded_ref):
    for i in range(ROWS // TILE):
        rows = slice(i * TILE, (i + 1) * TILE)
        folded = jnp.zeros((TILE, LANES), F32)
        for j in range(COLS // TILE):
            cols = slice(j * TILE, (j + 1) * TILE)
            scores = scores_ref[rows, cols] + lax.dot_general(
                src_last_ref[:, rows], block_ref[:, cols], CONTRACT, preferred_element_type=F32
            )
            live = live_ref[i, j][:1, :1] > 0.0
            part = jnp.where(live, jnp.exp(scores * SHARPNESS), 0.0)
            kernel_ref[rows, cols] = part
            for k in range(TILE // LANES):
                folded = folded + part[:, k * LANES : (k + 1) * LANES]
        folded_ref[rows, :] = folded
    own = mass_ref[...]
    sums = jnp.concatenate([lane_sums(folded_ref[...]), own, own], axis=0)
    sums_ref[...] = jnp.broadcast_to(sums[None], sums_ref.shape)


def first_columns_body(kernel_ref, parts_ref, mass_ref, out_ref):
    half = CHUNKS // 2
    mass = jnp.concatenate([parts_ref[k, CHUNKS : CHUNKS + half, :] for k in range(2)], axis=0)
    mass_ref[...] = mass
    column_sums(kernel_ref, mass / jnp.sum(parts_ref[:, :CHUNKS, :], axis=0), out_ref)


def columns_body(kernel_ref, parts_ref, mass_ref, out_ref):
    column_sums(kernel_ref, mass_ref[...] / jnp.sum(parts_ref[...], axis=0), out_ref)


def last_columns_body(kernel_ref, parts_ref, mass_ref, side_ref, log_ref, out_ref):
    scale = mass_ref[...] / jnp.sum(parts_ref[...], axis=0)
    log_ref[...] = jnp.log(
        jnp.where(side_ref[...] == 0.0, scale[: CHUNKS // 2], scale[CHUNKS // 2 :])
    )
    column_sums(kernel_ref, scale, out_ref)


def column_sums(kernel_ref, scale, out_ref):
    acc = [None] * (COLS // LANES)
    for i in range(CHUNKS):
        wide = jnp.broadcast_to(scale[i : i + 1, :], (LANES, LANES)).T
        for j in range(COLS // LANES):
            prod = kernel_ref[i * LANES : (i + 1) * LANES, j * LANES : (j + 1) * LANES] * wide
            prod = jnp.sum(prod.reshape(LANES // 8, 8, LANES), axis=0)
            acc[j] = prod if acc[j] is None else acc[j] + prod
    sums = jnp.concatenate([jnp.sum(a, axis=0, keepdims=True) for a in acc], axis=0)
    out_ref[...] = jnp.broadcast_to(sums[None], out_ref.shape)


def rows_body(kernel_ref, mass_ref, parts_ref, sums_ref, folded_ref):
    scale = mass_ref[...] / jnp.sum(parts_ref[...], axis=0)
    for i in range(CHUNKS):
        rows = slice(i * LANES, (i + 1) * LANES)
        total = kernel_ref[rows, :LANES] * scale[0:1, :]
        for j in range(1, COLS // LANES):
            total = total + kernel_ref[rows, j * LANES : (j + 1) * LANES] * scale[j : j + 1, :]
        folded_ref[rows, :] = total
    sums_ref[...] = jnp.broadcast_to(lane_sums(folded_ref[...])[None], sums_ref.shape)


HALF = jax.ShapeDtypeStruct((CHUNKS // 2, LANES), F32)
SMALL = jax.ShapeDtypeStruct((CHUNKS, LANES), F32)
WIDE = pltpu.VMEM((N_Z * N_Y, CHUNKS, LANES), F32)
RING = (2 * N_X, CHUNKS, LANES)
KERNEL = pltpu.VMEM((ROWS, COLS), F32)
BUILD = pltpu.CompilerParams(vmem_limit_bytes=28 * 1024 * 1024)
SWEEP = pltpu.CompilerParams(vmem_limit_bytes=16 * 1024 * 1024)


def shards(src_emb, tgt_emb, tile_mask, src_mass, tgt_mass):
    sent = pl.pallas_call(
        halves_body,
        out_shape=jax.ShapeDtypeStruct((2 * N_Y, GROUP, COLS), jnp.bfloat16),
        in_specs=[VMEM],
        out_specs=VMEM,
        compiler_params=SWEEP,
    )(tgt_emb[0])
    plane = lax.all_to_all(sent, ("y", "xl"), 0, 0, tiled=True).reshape(2 * N_Y * GROUP, COLS)
    src = src_emb[0]
    plane, one, two = lax.optimization_barrier((plane, wheel_x(src, 1), wheel_x(src, -1)))
    three = wheel_x(one, 1)
    swapped = [shift(s, "c", 2, 1) for s in (src, one, two)]
    blocks = [plane]
    near = away = plane
    for step in range(3):
        near, away = wheel(near, 1), wheel(away, -1)
        if step == 0:
            near, away, three, *swapped = lax.optimization_barrier((near, away, three, *swapped))
            swapped.append(shift(three, "c", 2, 1))
        if step == 1:
            near, away, swapped[3] = lax.optimization_barrier((near, away, swapped[3]))
        blocks += [near, away]
    far = wheel(near, 1)

    where = jnp.stack([lax.axis_index(a) for a in ("z", "c", "xh", "xl")]).astype(jnp.int32)
    scores, src_last, live, tgt_cols, side = pl.pallas_call(
        partial_body,
        out_shape=(
            KERNEL,
            pltpu.VMEM((LANES, ROWS), jnp.bfloat16),
            pltpu.VMEM((ROWS // TILE, COLS // TILE, 8, LANES), F32),
            SMALL,
            HALF,
        ),
        in_specs=[SMEM] + [HBM] * 3 + [VMEM] * (7 + len(blocks)),
        out_specs=(VMEM,) * 5,
        scratch_shapes=[
            pltpu.VMEM((VECTOR_DIMENSION, ROWS), jnp.bfloat16),
            pltpu.VMEM((VECTOR_DIMENSION, COLS), jnp.bfloat16),
            pltpu.SMEM(tile_mask.shape, jnp.int32),
            pltpu.VMEM((2 * CHUNKS, LANES), F32),
            pltpu.SemaphoreType.DMA((3,)),
        ],
        compiler_params=BUILD,
        cost_estimate=pl.CostEstimate(
            flops=2 * ROWS * COLS * VECTOR_DIMENSION, bytes_accessed=10_000_000, transcendentals=0
        ),
    )(where, *map(in_hbm, (tile_mask, tgt_mass.reshape(-1, LANES), src)), one, two, three, *swapped, *blocks)
    own = src_mass.reshape(-1, LANES)
    kernel, sums = pl.pallas_call(
        build_body,
        out_shape=(KERNEL, pltpu.VMEM((2 * N_X, 2 * CHUNKS, LANES), F32)),
        in_specs=[VMEM] * 5,
        out_specs=(VMEM, VMEM),
        scratch_shapes=[pltpu.VMEM((ROWS, LANES), F32)],
        compiler_params=BUILD,
    )(in_vmem(src_last), in_vmem(scores), in_vmem(live), own, far)

    kernel = in_vmem(kernel)
    for sweep in range(ITERS):
        parts = lax.all_to_all(sums, ("xh", "c", "xl"), 0, 0, tiled=True)
        if sweep == 0:
            body, operands, extra = first_columns_body, (), (SMALL,)
        elif sweep < ITERS - 1:
            body, operands, extra = columns_body, (mass,), ()
        else:
            body, operands, extra = last_columns_body, (mass, side), (HALF,)
        outs = pl.pallas_call(
            body,
            out_shape=(*extra, WIDE),
            in_specs=[VMEM] * (2 + len(operands)),
            out_specs=(VMEM,) * (1 + len(extra)),
            compiler_params=SWEEP,
        )(kernel, parts, *operands)
        if sweep == 0:
            mass = outs[0]
        parts = lax.all_to_all(outs[-1], PLANE, 0, 0, tiled=True)
        if sweep < ITERS - 1:
            sums = pl.pallas_call(
                rows_body,
                out_shape=pltpu.VMEM(RING, F32),
                in_specs=[VMEM] * 3,
                out_specs=VMEM,
                scratch_shapes=[pltpu.VMEM((ROWS, LANES), F32)],
                compiler_params=SWEEP,
            )(kernel, tgt_cols, parts)

    log_src = outs[0]
    mine = jnp.log(tgt_cols / jnp.sum(parts, axis=0)).reshape(-1)
    theirs = shift(mine, "xl", 2, 1)
    log_tgt = jnp.where(lax.axis_index("xl") == 0, jnp.concatenate([mine, theirs]), jnp.concatenate([theirs, mine]))
    return log_src.reshape(-1), log_tgt


def solution(mesh):
    fine = Mesh(mesh.devices.reshape(N_Z, N_Y, 2, 2, 2), ("z", "y", "xh", "c", "xl"))
    placed = (
        P("xl", ("xh", "c"), ("z", "y")),
        P("xl", ("z", "y"), ("xh", "c")),
        P(("z", "y"), ("xh", "c")),
        P(("z", "y", "xl")),
        P(("xh", "c")),
    )
    return jax.shard_map(
        shards,
        mesh=fine,
        in_specs=placed,
        out_specs=(P(("z", "y", "xl")), P(("xh", "c"))),
        check_vma=False,
    )
```

```python
import math

import jax
import jax.numpy as jnp
from jax import lax
from jax.experimental import pallas as pl
from jax.experimental.pallas import tpu as pltpu
from jax.sharding import Mesh
from jax.sharding import PartitionSpec as P

VECTOR_DIMENSION = 1024
TILE = 512
ITERS = 3
SHARPNESS = 1.0 / (0.64 * math.sqrt(VECTOR_DIMENSION))

X = ("xh", "xl")
PLANE = ("z", "y")
N_Z, N_Y, N_X = 8, 4, 4
ROWS = 1024
COLS = 1024
LANES = 128
CHUNKS = ROWS // LANES
GROUP = 16
F32 = jnp.float32
VMEM = pl.BlockSpec(memory_space=pltpu.VMEM)
HBM = pl.BlockSpec(memory_space=pltpu.HBM)
SMEM = pl.BlockSpec(memory_space=pltpu.SMEM)


def shift(value, axis, size, by):
    return lax.ppermute(value, axis, [(i, (i + by) % size) for i in range(size)])


def wheel_y(value, by):
    pairs = [
        (i * 2 + c, (i + (by if c == 0 else -by)) % N_Y * 2 + c) for i in range(N_Y) for c in range(2)
    ]
    return lax.ppermute(value, ("y", "c"), pairs)


def wheel_x(value, by):
    place = lambda x, c: x // 2 * 4 + c * 2 + x % 2
    pairs = [
        (place(i, c), place((i + (by if c == 0 else -by)) % N_X, c)) for i in range(N_X) for c in range(2)
    ]
    return lax.ppermute(value, ("xh", "c", "xl"), pairs)


def in_vmem(value):
    return pltpu.with_memory_space_constraint(value, pltpu.VMEM)


def in_hbm(value):
    return pltpu.with_memory_space_constraint(value, pltpu.HBM)


def lane_sums(folded):
    parts = [
        jnp.sum(folded[i * LANES : (i + 1) * LANES, :].T, axis=0, keepdims=True)
        for i in range(folded.shape[0] // LANES)
    ]
    return jnp.concatenate(parts, axis=0)


def turned(value, size):
    return lax.rem(value + size, size)


CONTRACT = (((0,), (0,)), ((), ()))
TURNS = (0, -1, 1, 2)
BAND = 2 * N_Z * GROUP


def halves_body(tgt_ref, out_ref):
    for z in range(N_Z):
        for low in range(2):
            out_ref[z * 2 + low] = tgt_ref[:, low * COLS : (low + 1) * COLS]


def prepare_body(where_ref, mask_hbm, tgt_mass_hbm, src_hbm, *refs):
    src_refs, block_ref = refs[:7], refs[7]
    scores_ref, ordered_ref, live_ref, tgt_cols_ref, side_ref = refs[8:13]
    src_ref, mask_ref, tgt_mass_ref, sems = refs[13:]
    y, c, xh, xl = (where_ref[i] for i in range(4))

    def src_at(core, turn):
        x = turned(xh * 2 + xl + turn * (1 - 2 * core), N_X)
        to = lax.rem(x, 2) * 512 + lax.div(x, 2) * 256 + core * 128
        return src_ref.at[pl.ds(pl.multiple_of(to, LANES), LANES), :]

    fetches = [
        pltpu.make_async_copy(src_hbm, src_at(c, 0), sems.at[0]),
        pltpu.make_async_copy(mask_hbm, mask_ref, sems.at[1]),
        pltpu.make_async_copy(tgt_mass_hbm, tgt_mass_ref, sems.at[2]),
    ]
    for fetch in fetches:
        fetch.start()
    for index, part in enumerate(src_refs):
        core, turn = (c, index + 1) if index < 3 else (1 - c, index - 3)
        src_at(core, TURNS[turn])[...] = part[...]
    for fetch in fetches:
        fetch.wait()
    for band, turn in enumerate(TURNS):
        at_y = turned(y + turn * (1 - 2 * c), N_Y)
        for z in range(N_Z):
            for low in range(2):
                to = band * BAND + (z * 2 + low) * GROUP
                at = pl.multiple_of(low * 512 + z * (N_Y * GROUP) + at_y * GROUP, GROUP)
                ordered_ref[to : to + GROUP, :] = src_ref[pl.ds(at, GROUP), :]
    tgt_cols_ref[...] = jnp.where(xl == 0, tgt_mass_ref[:CHUNKS, :], tgt_mass_ref[CHUNKS:, :])
    side_ref[...] = jnp.full(side_ref.shape, xl.astype(F32))
    for i in range(ROWS // TILE):
        rows = slice(i * TILE, (i + 1) * TILE)
        for j in range(COLS // TILE):
            cols = slice(j * TILE, (j + 1) * TILE)
            live = mask_ref[i, xl * (COLS // TILE) + j] > 0
            live_ref[i, j] = jnp.full((8, LANES), live.astype(F32))
            scores_ref[rows, cols] = band_scores(ordered_ref, 0, block_ref, rows, cols)


def band_scores(ordered_ref, band, block_ref, rows, cols):
    return lax.dot_general(
        ordered_ref[band * BAND : (band + 1) * BAND, rows],
        block_ref[:, cols],
        CONTRACT,
        preferred_element_type=F32,
    )


def partial_body(ordered_ref, scores_ref, near_ref, away_ref, out_ref):
    for i in range(ROWS // TILE):
        rows = slice(i * TILE, (i + 1) * TILE)
        for j in range(COLS // TILE):
            cols = slice(j * TILE, (j + 1) * TILE)
            out_ref[rows, cols] = (
                scores_ref[rows, cols]
                + band_scores(ordered_ref, 1, near_ref, rows, cols)
                + band_scores(ordered_ref, 2, away_ref, rows, cols)
            )


def build_body(ordered_ref, scores_ref, live_ref, mass_ref, far_ref, kernel_ref, sums_ref, folded_ref):
    for i in range(ROWS // TILE):
        rows = slice(i * TILE, (i + 1) * TILE)
        folded = jnp.zeros((TILE, LANES), F32)
        for j in range(COLS // TILE):
            cols = slice(j * TILE, (j + 1) * TILE)
            scores = scores_ref[rows, cols] + band_scores(ordered_ref, 3, far_ref, rows, cols)
            live = live_ref[i, j][:1, :1] > 0.0
            part = jnp.where(live, jnp.exp(scores * SHARPNESS), 0.0)
            kernel_ref[rows, cols] = part
            for k in range(TILE // LANES):
                folded = folded + part[:, k * LANES : (k + 1) * LANES]
        folded_ref[rows, :] = folded
    own = mass_ref[...]
    sums = jnp.concatenate([lane_sums(folded_ref[...]), own, own], axis=0)
    sums_ref[...] = jnp.broadcast_to(sums[None], sums_ref.shape)


def first_columns_body(kernel_ref, parts_ref, mass_ref, out_ref):
    half = CHUNKS // 2
    mass = jnp.concatenate([parts_ref[k, CHUNKS : CHUNKS + half, :] for k in range(2)], axis=0)
    mass_ref[...] = mass
    column_sums(kernel_ref, mass / jnp.sum(parts_ref[:, :CHUNKS, :], axis=0), out_ref)


def columns_body(kernel_ref, parts_ref, mass_ref, out_ref):
    column_sums(kernel_ref, mass_ref[...] / jnp.sum(parts_ref[...], axis=0), out_ref)


def last_columns_body(kernel_ref, parts_ref, mass_ref, side_ref, log_ref, out_ref):
    scale = mass_ref[...] / jnp.sum(parts_ref[...], axis=0)
    log_ref[...] = jnp.log(
        jnp.where(side_ref[...] == 0.0, scale[: CHUNKS // 2], scale[CHUNKS // 2 :])
    )
    column_sums(kernel_ref, scale, out_ref)


def column_sums(kernel_ref, scale, out_ref):
    acc = [None] * (COLS // LANES)
    for i in range(CHUNKS):
        wide = jnp.broadcast_to(scale[i : i + 1, :], (LANES, LANES)).T
        for j in range(COLS // LANES):
            prod = kernel_ref[i * LANES : (i + 1) * LANES, j * LANES : (j + 1) * LANES] * wide
            prod = jnp.sum(prod.reshape(LANES // 8, 8, LANES), axis=0)
            acc[j] = prod if acc[j] is None else acc[j] + prod
    sums = jnp.concatenate([jnp.sum(a, axis=0, keepdims=True) for a in acc], axis=0)
    out_ref[...] = jnp.broadcast_to(sums[None], out_ref.shape)


def rows_body(kernel_ref, mass_ref, parts_ref, sums_ref, folded_ref):
    scale = mass_ref[...] / jnp.sum(parts_ref[...], axis=0)
    for i in range(CHUNKS):
        rows = slice(i * LANES, (i + 1) * LANES)
        total = kernel_ref[rows, :LANES] * scale[0:1, :]
        for j in range(1, COLS // LANES):
            total = total + kernel_ref[rows, j * LANES : (j + 1) * LANES] * scale[j : j + 1, :]
        folded_ref[rows, :] = total
    sums_ref[...] = jnp.broadcast_to(lane_sums(folded_ref[...])[None], sums_ref.shape)


HALF = jax.ShapeDtypeStruct((CHUNKS // 2, LANES), F32)
SMALL = jax.ShapeDtypeStruct((CHUNKS, LANES), F32)
WIDE = pltpu.VMEM((N_Z * N_Y, CHUNKS, LANES), F32)
RING = (2 * N_X, CHUNKS, LANES)
KERNEL = pltpu.VMEM((ROWS, COLS), F32)
BUILD = pltpu.CompilerParams(vmem_limit_bytes=28 * 1024 * 1024)
SWEEP = pltpu.CompilerParams(vmem_limit_bytes=16 * 1024 * 1024)


def work(bands):
    return pl.CostEstimate(
        flops=2 * ROWS * COLS * BAND * bands, bytes_accessed=8_000_000, transcendentals=0
    )


def shards(src_emb, tgt_emb, tile_mask, src_mass, tgt_mass):
    src = src_emb[0]
    src_a = [wheel_x(src, 1), wheel_x(src, -1), wheel_x(src, 2)]
    sent = pl.pallas_call(
        halves_body,
        out_shape=jax.ShapeDtypeStruct((2 * N_Z, GROUP, COLS), jnp.bfloat16),
        in_specs=[VMEM],
        out_specs=VMEM,
        compiler_params=SWEEP,
    )(tgt_emb[0])
    own_band = lax.all_to_all(sent, ("z", "xl"), 0, 0, tiled=True).reshape(BAND, COLS)
    swapped = [shift(s, "c", 2, 1) for s in (src, *src_a)]
    near, away = wheel_y(own_band, 1), wheel_y(own_band, -1)
    near, *swapped = lax.optimization_barrier((near, *swapped))
    far = wheel_y(near, 1)

    where = jnp.stack([lax.axis_index(a) for a in ("y", "c", "xh", "xl")]).astype(jnp.int32)
    scores, ordered, live, tgt_cols, side = pl.pallas_call(
        prepare_body,
        out_shape=(
            KERNEL,
            pltpu.VMEM((VECTOR_DIMENSION, ROWS), jnp.bfloat16),
            pltpu.VMEM((ROWS // TILE, COLS // TILE, 8, LANES), F32),
            SMALL,
            HALF,
        ),
        in_specs=[SMEM] + [HBM] * 3 + [VMEM] * 8,
        out_specs=(VMEM,) * 5,
        scratch_shapes=[
            pltpu.VMEM((VECTOR_DIMENSION, ROWS), jnp.bfloat16),
            pltpu.SMEM(tile_mask.shape, jnp.int32),
            pltpu.VMEM((2 * CHUNKS, LANES), F32),
            pltpu.SemaphoreType.DMA((3,)),
        ],
        compiler_params=BUILD,
        cost_estimate=work(1),
    )(where, *map(in_hbm, (tile_mask, tgt_mass.reshape(-1, LANES), src)), *src_a, *swapped, own_band)
    ordered = in_vmem(ordered)
    scores = pl.pallas_call(
        partial_body,
        out_shape=KERNEL,
        in_specs=[VMEM] * 4,
        out_specs=VMEM,
        compiler_params=BUILD,
        cost_estimate=work(2),
    )(ordered, in_vmem(scores), near, away)
    own = src_mass.reshape(-1, LANES)
    kernel, sums = pl.pallas_call(
        build_body,
        out_shape=(KERNEL, pltpu.VMEM((2 * N_X, 2 * CHUNKS, LANES), F32)),
        in_specs=[VMEM] * 5,
        out_specs=(VMEM, VMEM),
        scratch_shapes=[pltpu.VMEM((ROWS, LANES), F32)],
        compiler_params=BUILD,
        cost_estimate=work(1),
    )(ordered, in_vmem(scores), in_vmem(live), own, far)

    kernel = in_vmem(kernel)
    for sweep in range(ITERS):
        parts = lax.all_to_all(sums, ("xh", "c", "xl"), 0, 0, tiled=True)
        if sweep == 0:
            body, operands, extra = first_columns_body, (), (SMALL,)
        elif sweep < ITERS - 1:
            body, operands, extra = columns_body, (mass,), ()
        else:
            body, operands, extra = last_columns_body, (mass, side), (HALF,)
        outs = pl.pallas_call(
            body,
            out_shape=(*extra, WIDE),
            in_specs=[VMEM] * (2 + len(operands)),
            out_specs=(VMEM,) * (1 + len(extra)),
            compiler_params=SWEEP,
        )(kernel, parts, *operands)
        if sweep == 0:
            mass = outs[0]
        parts = lax.all_to_all(outs[-1], PLANE, 0, 0, tiled=True)
        if sweep < ITERS - 1:
            sums = pl.pallas_call(
                rows_body,
                out_shape=pltpu.VMEM(RING, F32),
                in_specs=[VMEM] * 3,
                out_specs=VMEM,
                scratch_shapes=[pltpu.VMEM((ROWS, LANES), F32)],
                compiler_params=SWEEP,
            )(kernel, tgt_cols, parts)

    log_src = outs[0]
    mine = jnp.log(tgt_cols / jnp.sum(parts, axis=0)).reshape(-1)
    theirs = shift(mine, "xl", 2, 1)
    log_tgt = jnp.where(lax.axis_index("xl") == 0, jnp.concatenate([mine, theirs]), jnp.concatenate([theirs, mine]))
    return log_src.reshape(-1), log_tgt


def solution(mesh):
    fine = Mesh(mesh.devices.reshape(N_Z, N_Y, 2, 2, 2), ("z", "y", "xh", "c", "xl"))
    placed = (
        P("xl", ("xh", "c"), ("z", "y")),
        P("xl", ("z", "y"), ("xh", "c")),
        P(("z", "y"), ("xh", "c")),
        P(("z", "y", "xl")),
        P(("xh", "c")),
    )
    return jax.shard_map(
        shards,
        mesh=fine,
        in_specs=placed,
        out_specs=(P(("z", "y", "xl")), P(("xh", "c"))),
        check_vma=False,
    )
```

```python
import math

import jax
import jax.numpy as jnp
from jax import lax
from jax.experimental import pallas as pl
from jax.experimental.pallas import tpu as pltpu
from jax.sharding import Mesh
from jax.sharding import PartitionSpec as P

VECTOR_DIMENSION = 1024
TILE = 512
ITERS = 3
SHARPNESS = 1.0 / (0.64 * math.sqrt(VECTOR_DIMENSION))

X = ("xh", "xl")
PLANE = ("z", "y")
N_Z, N_Y, N_X = 8, 4, 4
ROWS = 1024
COLS = 1024
LANES = 128
CHUNKS = ROWS // LANES
GROUP = 16
F32 = jnp.float32
VMEM = pl.BlockSpec(memory_space=pltpu.VMEM)
HBM = pl.BlockSpec(memory_space=pltpu.HBM)
SMEM = pl.BlockSpec(memory_space=pltpu.SMEM)


def shift(value, axis, size, by):
    return lax.ppermute(value, axis, [(i, (i + by) % size) for i in range(size)])


def wheel_y(value, by):
    pairs = [
        (i * 2 + c, (i + (by if c == 0 else -by)) % N_Y * 2 + c) for i in range(N_Y) for c in range(2)
    ]
    return lax.ppermute(value, ("y", "c"), pairs)


def wheel_x(value, by):
    place = lambda x, c: x // 2 * 4 + c * 2 + x % 2
    pairs = [
        (place(i, c), place((i + (by if c == 0 else -by)) % N_X, c)) for i in range(N_X) for c in range(2)
    ]
    return lax.ppermute(value, ("xh", "c", "xl"), pairs)


def ring_parts(sums):
    chip = sums + shift(sums, "c", 2, 1)
    one, far = wheel_x(chip, 1), shift(chip, X, N_X, 2)
    return [chip, one, far, shift(one, "c", 2, 1)]


def in_vmem(value):
    return pltpu.with_memory_space_constraint(value, pltpu.VMEM)


def in_hbm(value):
    return pltpu.with_memory_space_constraint(value, pltpu.HBM)


def lane_sums(folded):
    parts = [
        jnp.sum(folded[i * LANES : (i + 1) * LANES, :].T, axis=0, keepdims=True)
        for i in range(folded.shape[0] // LANES)
    ]
    return jnp.concatenate(parts, axis=0)


def turned(value, size):
    return lax.rem(value + size, size)


CONTRACT = (((0,), (0,)), ((), ()))
TURNS = (0, -1, 1, 2)
BAND = 2 * N_Z * GROUP


def halves_body(tgt_ref, out_ref):
    for z in range(N_Z):
        for low in range(2):
            out_ref[z * 2 + low] = tgt_ref[:, low * COLS : (low + 1) * COLS]


def prepare_body(where_ref, mask_hbm, tgt_mass_hbm, src_hbm, *refs):
    src_refs, block_ref = refs[:7], refs[7]
    scores_ref, ordered_ref, live_ref, tgt_cols_ref, side_ref = refs[8:13]
    src_ref, mask_ref, tgt_mass_ref, sems = refs[13:]
    y, c, xh, xl = (where_ref[i] for i in range(4))

    def src_at(core, turn):
        x = turned(xh * 2 + xl + turn * (1 - 2 * core), N_X)
        to = lax.rem(x, 2) * 512 + lax.div(x, 2) * 256 + core * 128
        return src_ref.at[pl.ds(pl.multiple_of(to, LANES), LANES), :]

    fetches = [
        pltpu.make_async_copy(src_hbm, src_at(c, 0), sems.at[0]),
        pltpu.make_async_copy(mask_hbm, mask_ref, sems.at[1]),
        pltpu.make_async_copy(tgt_mass_hbm, tgt_mass_ref, sems.at[2]),
    ]
    for fetch in fetches:
        fetch.start()
    for index, part in enumerate(src_refs):
        core, turn = (c, index + 1) if index < 3 else (1 - c, index - 3)
        src_at(core, TURNS[turn])[...] = part[...]
    for fetch in fetches:
        fetch.wait()
    for band, turn in enumerate(TURNS):
        at_y = turned(y + turn * (1 - 2 * c), N_Y)
        for z in range(N_Z):
            for low in range(2):
                to = band * BAND + (z * 2 + low) * GROUP
                at = pl.multiple_of(low * 512 + z * (N_Y * GROUP) + at_y * GROUP, GROUP)
                ordered_ref[to : to + GROUP, :] = src_ref[pl.ds(at, GROUP), :]
    tgt_cols_ref[...] = jnp.where(xl == 0, tgt_mass_ref[:CHUNKS, :], tgt_mass_ref[CHUNKS:, :])
    side_ref[...] = jnp.full(side_ref.shape, xl.astype(F32))
    for i in range(ROWS // TILE):
        rows = slice(i * TILE, (i + 1) * TILE)
        for j in range(COLS // TILE):
            cols = slice(j * TILE, (j + 1) * TILE)
            live = mask_ref[i, xl * (COLS // TILE) + j] > 0
            live_ref[i, j] = jnp.full((8, LANES), live.astype(F32))
            scores_ref[rows, cols] = band_scores(ordered_ref, 0, block_ref, rows, cols)


def band_scores(ordered_ref, band, block_ref, rows, cols):
    return lax.dot_general(
        ordered_ref[band * BAND : (band + 1) * BAND, rows],
        block_ref[:, cols],
        CONTRACT,
        preferred_element_type=F32,
    )


def split_body(band_ref, first_ref, second_ref):
    first_ref[...] = band_ref[: BAND // 2, :]
    second_ref[...] = band_ref[BAND // 2 :, :]


def joined(ref, halves):
    for k, half in enumerate(halves):
        ref[k * BAND // 2 : (k + 1) * BAND // 2, :] = half[...]


def partial_body(ordered_ref, scores_ref, near_0_ref, near_1_ref, away_ref, out_ref, near_ref):
    joined(near_ref, (near_0_ref, near_1_ref))
    for i in range(ROWS // TILE):
        rows = slice(i * TILE, (i + 1) * TILE)
        for j in range(COLS // TILE):
            cols = slice(j * TILE, (j + 1) * TILE)
            out_ref[rows, cols] = (
                scores_ref[rows, cols]
                + band_scores(ordered_ref, 1, near_ref, rows, cols)
                + band_scores(ordered_ref, 2, away_ref, rows, cols)
            )


def build_body(
    ordered_ref, scores_ref, live_ref, mass_ref, far_0_ref, far_1_ref, kernel_ref, sums_ref, folded_ref, far_ref
):
    joined(far_ref, (far_0_ref, far_1_ref))
    for i in range(ROWS // TILE):
        rows = slice(i * TILE, (i + 1) * TILE)
        folded = jnp.zeros((TILE, LANES), F32)
        for j in range(COLS // TILE):
            cols = slice(j * TILE, (j + 1) * TILE)
            scores = scores_ref[rows, cols] + band_scores(ordered_ref, 3, far_ref, rows, cols)
            live = live_ref[i, j][:1, :1] > 0.0
            part = jnp.where(live, jnp.exp(scores * SHARPNESS), 0.0)
            kernel_ref[rows, cols] = part
            for k in range(TILE // LANES):
                folded = folded + part[:, k * LANES : (k + 1) * LANES]
        folded_ref[rows, :] = folded
    own = mass_ref[...]
    sums = jnp.concatenate([lane_sums(folded_ref[...]), own, own], axis=0)
    sums_ref[...] = jnp.broadcast_to(sums[None], sums_ref.shape)


def first_columns_body(kernel_ref, parts_ref, mass_ref, out_ref):
    half = CHUNKS // 2
    mass = jnp.concatenate([parts_ref[k, CHUNKS : CHUNKS + half, :] for k in range(2)], axis=0)
    mass_ref[...] = mass
    column_sums(kernel_ref, mass / jnp.sum(parts_ref[:, :CHUNKS, :], axis=0), out_ref)


def columns_body(kernel_ref, mass_ref, *refs):
    part_refs, out_ref = refs[:4], refs[4]
    total = sum(part[...] for part in part_refs)
    column_sums(kernel_ref, mass_ref[...] / total, out_ref)


def last_columns_body(kernel_ref, mass_ref, side_ref, *refs):
    part_refs, (log_ref, out_ref) = refs[:4], refs[4:]
    scale = mass_ref[...] / sum(part[...] for part in part_refs)
    log_ref[...] = jnp.log(
        jnp.where(side_ref[...] == 0.0, scale[: CHUNKS // 2], scale[CHUNKS // 2 :])
    )
    column_sums(kernel_ref, scale, out_ref)


def column_sums(kernel_ref, scale, out_ref):
    acc = [None] * (COLS // LANES)
    for i in range(CHUNKS):
        wide = jnp.broadcast_to(scale[i : i + 1, :], (LANES, LANES)).T
        for j in range(COLS // LANES):
            prod = kernel_ref[i * LANES : (i + 1) * LANES, j * LANES : (j + 1) * LANES] * wide
            prod = jnp.sum(prod.reshape(LANES // 8, 8, LANES), axis=0)
            acc[j] = prod if acc[j] is None else acc[j] + prod
    sums = jnp.concatenate([jnp.sum(a, axis=0, keepdims=True) for a in acc], axis=0)
    out_ref[...] = jnp.broadcast_to(sums[None], out_ref.shape)


def rows_body(kernel_ref, mass_ref, parts_ref, sums_ref, folded_ref):
    scale = mass_ref[...] / jnp.sum(parts_ref[...], axis=0)
    for i in range(CHUNKS):
        rows = slice(i * LANES, (i + 1) * LANES)
        total = kernel_ref[rows, :LANES] * scale[0:1, :]
        for j in range(1, COLS // LANES):
            total = total + kernel_ref[rows, j * LANES : (j + 1) * LANES] * scale[j : j + 1, :]
        folded_ref[rows, :] = total
    sums_ref[...] = lane_sums(folded_ref[...])


HALF = jax.ShapeDtypeStruct((CHUNKS // 2, LANES), F32)
SMALL = jax.ShapeDtypeStruct((CHUNKS, LANES), F32)
WIDE = pltpu.VMEM((N_Z * N_Y, CHUNKS, LANES), F32)
RING = (2 * N_X, CHUNKS, LANES)
KERNEL = pltpu.VMEM((ROWS, COLS), F32)
HALF_BAND = pltpu.VMEM((N_Z * GROUP, COLS), jnp.bfloat16)
BUILD = pltpu.CompilerParams(vmem_limit_bytes=28 * 1024 * 1024)
SWEEP = pltpu.CompilerParams(vmem_limit_bytes=16 * 1024 * 1024)


def work(bands):
    return pl.CostEstimate(
        flops=2 * ROWS * COLS * BAND * bands, bytes_accessed=8_000_000, transcendentals=0
    )


def shards(src_emb, tgt_emb, tile_mask, src_mass, tgt_mass):
    src = src_emb[0]
    src_a = [wheel_x(src, 1), wheel_x(src, -1), wheel_x(src, 2)]
    sent = pl.pallas_call(
        halves_body,
        out_shape=jax.ShapeDtypeStruct((2 * N_Z, GROUP, COLS), jnp.bfloat16),
        in_specs=[VMEM],
        out_specs=VMEM,
        compiler_params=SWEEP,
    )(tgt_emb[0])
    own_band = lax.all_to_all(sent, ("z", "xl"), 0, 0, tiled=True).reshape(BAND, COLS)
    split_band = pl.pallas_call(
        split_body,
        out_shape=(HALF_BAND, HALF_BAND),
        in_specs=[VMEM],
        out_specs=(VMEM, VMEM),
        compiler_params=SWEEP,
    )(own_band)
    swapped = [shift(s, "c", 2, 1) for s in (src, *src_a[:2])]
    near = [wheel_y(v, 1) for v in split_band]
    away = wheel_y(own_band, -1)
    late, _ = lax.optimization_barrier((src_a[2], near[0]))
    swapped.append(shift(late, "c", 2, 1))
    far = [wheel_y(v, 1) for v in near]

    where = jnp.stack([lax.axis_index(a) for a in ("y", "c", "xh", "xl")]).astype(jnp.int32)
    scores, ordered, live, tgt_cols, side = pl.pallas_call(
        prepare_body,
        out_shape=(
            KERNEL,
            pltpu.VMEM((VECTOR_DIMENSION, ROWS), jnp.bfloat16),
            pltpu.VMEM((ROWS // TILE, COLS // TILE, 8, LANES), F32),
            SMALL,
            HALF,
        ),
        in_specs=[SMEM] + [HBM] * 3 + [VMEM] * 8,
        out_specs=(VMEM,) * 5,
        scratch_shapes=[
            pltpu.VMEM((VECTOR_DIMENSION, ROWS), jnp.bfloat16),
            pltpu.SMEM(tile_mask.shape, jnp.int32),
            pltpu.VMEM((2 * CHUNKS, LANES), F32),
            pltpu.SemaphoreType.DMA((3,)),
        ],
        compiler_params=BUILD,
        cost_estimate=work(1),
    )(where, *map(in_hbm, (tile_mask, tgt_mass.reshape(-1, LANES), src)), *src_a, *swapped, own_band)
    ordered = in_vmem(ordered)
    scores = pl.pallas_call(
        partial_body,
        out_shape=KERNEL,
        in_specs=[VMEM] * 5,
        out_specs=VMEM,
        scratch_shapes=[pltpu.VMEM((BAND, COLS), jnp.bfloat16)],
        compiler_params=BUILD,
        cost_estimate=work(2),
    )(ordered, in_vmem(scores), *near, away)
    own = src_mass.reshape(-1, LANES)
    kernel, sums = pl.pallas_call(
        build_body,
        out_shape=(KERNEL, pltpu.VMEM((2 * N_X, 2 * CHUNKS, LANES), F32)),
        in_specs=[VMEM] * 6,
        out_specs=(VMEM, VMEM),
        scratch_shapes=[pltpu.VMEM((ROWS, LANES), F32), pltpu.VMEM((BAND, COLS), jnp.bfloat16)],
        compiler_params=BUILD,
        cost_estimate=work(1),
    )(ordered, in_vmem(scores), in_vmem(live), own, *far)

    kernel = in_vmem(kernel)
    for sweep in range(ITERS):
        if sweep == 0:
            parts = [lax.all_to_all(sums, ("xh", "c", "xl"), 0, 0, tiled=True)]
        else:
            parts = ring_parts(sums)
        if sweep == 0:
            body, operands, extra = first_columns_body, (), (SMALL,)
        elif sweep < ITERS - 1:
            body, operands, extra = columns_body, (mass,), ()
        else:
            body, operands, extra = last_columns_body, (mass, side), (HALF,)
        outs = pl.pallas_call(
            body,
            out_shape=(*extra, WIDE),
            in_specs=[VMEM] * (1 + len(operands) + len(parts)),
            out_specs=(VMEM,) * (1 + len(extra)),
            compiler_params=SWEEP,
        )(kernel, *operands, *parts)
        if sweep == 0:
            mass = outs[0]
        parts = lax.all_to_all(outs[-1], PLANE, 0, 0, tiled=True)
        if sweep < ITERS - 1:
            sums = pl.pallas_call(
                rows_body,
                out_shape=SMALL,
                in_specs=[VMEM] * 3,
                out_specs=VMEM,
                scratch_shapes=[pltpu.VMEM((ROWS, LANES), F32)],
                compiler_params=SWEEP,
            )(kernel, tgt_cols, parts)

    log_src = outs[0]
    mine = jnp.log(tgt_cols / jnp.sum(parts, axis=0)).reshape(-1)
    theirs = shift(mine, "xl", 2, 1)
    log_tgt = jnp.where(lax.axis_index("xl") == 0, jnp.concatenate([mine, theirs]), jnp.concatenate([theirs, mine]))
    return log_src.reshape(-1), log_tgt


def solution(mesh):
    fine = Mesh(mesh.devices.reshape(N_Z, N_Y, 2, 2, 2), ("z", "y", "xh", "c", "xl"))
    placed = (
        P("xl", ("xh", "c"), ("z", "y")),
        P("xl", ("z", "y"), ("xh", "c")),
        P(("z", "y"), ("xh", "c")),
        P(("z", "y", "xl")),
        P(("xh", "c")),
    )
    return jax.shard_map(
        shards,
        mesh=fine,
        in_specs=placed,
        out_specs=(P(("z", "y", "xl")), P(("xh", "c"))),
        check_vma=False,
    )
```

```python
import math

import jax
import jax.numpy as jnp
from jax import lax
from jax.experimental import pallas as pl
from jax.experimental.pallas import tpu as pltpu
from jax.sharding import Mesh
from jax.sharding import PartitionSpec as P

VECTOR_DIMENSION = 1024
TILE = 512
ITERS = 3
SHARPNESS = 1.0 / (0.64 * math.sqrt(VECTOR_DIMENSION))

X = ("xh", "xl")
PLANE = ("z", "y")
N_Z, N_Y, N_X = 8, 4, 4
ROWS = 1024
COLS = 1024
LANES = 128
CHUNKS = ROWS // LANES
GROUP = 16
F32 = jnp.float32
VMEM = pl.BlockSpec(memory_space=pltpu.VMEM)
HBM = pl.BlockSpec(memory_space=pltpu.HBM)
SMEM = pl.BlockSpec(memory_space=pltpu.SMEM)


def shift(value, axis, size, by):
    return lax.ppermute(value, axis, [(i, (i + by) % size) for i in range(size)])


def wheel_y(value, by):
    pairs = [
        (i * 2 + c, (i + (by if c == 0 else -by)) % N_Y * 2 + c) for i in range(N_Y) for c in range(2)
    ]
    return lax.ppermute(value, ("y", "c"), pairs)


def wheel_x(value, by):
    place = lambda x, c: x // 2 * 4 + c * 2 + x % 2
    pairs = [
        (place(i, c), place((i + (by if c == 0 else -by)) % N_X, c)) for i in range(N_X) for c in range(2)
    ]
    return lax.ppermute(value, ("xh", "c", "xl"), pairs)


def ring_parts(sums):
    chip = sums + shift(sums, "c", 2, 1)
    one, far = wheel_x(chip, 1), shift(chip, X, N_X, 2)
    return [chip, one, far, shift(one, "c", 2, 1)]


def in_vmem(value):
    return pltpu.with_memory_space_constraint(value, pltpu.VMEM)


def in_hbm(value):
    return pltpu.with_memory_space_constraint(value, pltpu.HBM)


def lane_sums(folded):
    parts = [
        jnp.sum(folded[i * LANES : (i + 1) * LANES, :].T, axis=0, keepdims=True)
        for i in range(folded.shape[0] // LANES)
    ]
    return jnp.concatenate(parts, axis=0)


def turned(value, size):
    return lax.rem(value + size, size)


CONTRACT = (((0,), (0,)), ((), ()))
TURNS = (0, -1, 1, 2)
BAND = 2 * N_Z * GROUP


def halves_body(tgt_ref, out_ref):
    for z in range(N_Z):
        for low in range(2):
            out_ref[z * 2 + low] = tgt_ref[:, low * COLS : (low + 1) * COLS]


def prepare_body(where_ref, mask_hbm, tgt_mass_hbm, src_hbm, *refs):
    src_refs, block_ref = refs[:7], refs[7]
    scores_ref, ordered_ref, live_ref, tgt_cols_ref, side_ref = refs[8:13]
    src_ref, mask_ref, tgt_mass_ref, sems = refs[13:]
    y, c, xh, xl = (where_ref[i] for i in range(4))

    def src_at(core, turn):
        x = turned(xh * 2 + xl + turn * (1 - 2 * core), N_X)
        to = lax.rem(x, 2) * 512 + lax.div(x, 2) * 256 + core * 128
        return src_ref.at[pl.ds(pl.multiple_of(to, LANES), LANES), :]

    fetches = [
        pltpu.make_async_copy(src_hbm, src_at(c, 0), sems.at[0]),
        pltpu.make_async_copy(mask_hbm, mask_ref, sems.at[1]),
        pltpu.make_async_copy(tgt_mass_hbm, tgt_mass_ref, sems.at[2]),
    ]
    for fetch in fetches:
        fetch.start()
    for index, part in enumerate(src_refs):
        core, turn = (c, index + 1) if index < 3 else (1 - c, index - 3)
        src_at(core, TURNS[turn])[...] = part[...]
    for fetch in fetches:
        fetch.wait()
    for band, turn in enumerate(TURNS):
        at_y = turned(y + turn * (1 - 2 * c), N_Y)
        for z in range(N_Z):
            for low in range(2):
                to = band * BAND + (z * 2 + low) * GROUP
                at = pl.multiple_of(low * 512 + z * (N_Y * GROUP) + at_y * GROUP, GROUP)
                ordered_ref[to : to + GROUP, :] = src_ref[pl.ds(at, GROUP), :]
    tgt_cols_ref[...] = jnp.where(xl == 0, tgt_mass_ref[:CHUNKS, :], tgt_mass_ref[CHUNKS:, :])
    side_ref[...] = jnp.full(side_ref.shape, xl.astype(F32))
    for i in range(ROWS // TILE):
        rows = slice(i * TILE, (i + 1) * TILE)
        for j in range(COLS // TILE):
            cols = slice(j * TILE, (j + 1) * TILE)
            live = mask_ref[i, xl * (COLS // TILE) + j] > 0
            live_ref[i, j] = jnp.full((8, LANES), live.astype(F32))
            scores_ref[rows, cols] = band_scores(ordered_ref, 0, block_ref, rows, cols)


def band_scores(ordered_ref, band, block_ref, rows, cols):
    return lax.dot_general(
        ordered_ref[band * BAND : (band + 1) * BAND, rows],
        block_ref[:, cols],
        CONTRACT,
        preferred_element_type=F32,
    )


def split_body(band_ref, first_ref, second_ref):
    first_ref[...] = band_ref[: BAND // 2, :]
    second_ref[...] = band_ref[BAND // 2 :, :]


def joined(ref, halves):
    for k, half in enumerate(halves):
        ref[k * BAND // 2 : (k + 1) * BAND // 2, :] = half[...]


def partial_body(ordered_ref, scores_ref, near_0_ref, near_1_ref, away_ref, out_ref, near_ref):
    joined(near_ref, (near_0_ref, near_1_ref))
    for i in range(ROWS // TILE):
        rows = slice(i * TILE, (i + 1) * TILE)
        for j in range(COLS // TILE):
            cols = slice(j * TILE, (j + 1) * TILE)
            out_ref[rows, cols] = (
                scores_ref[rows, cols]
                + band_scores(ordered_ref, 1, near_ref, rows, cols)
                + band_scores(ordered_ref, 2, away_ref, rows, cols)
            )


def build_body(
    ordered_ref, scores_ref, live_ref, mass_ref, far_0_ref, far_1_ref, kernel_ref, sums_ref, folded_ref, far_ref
):
    joined(far_ref, (far_0_ref, far_1_ref))
    for i in range(ROWS // TILE):
        rows = slice(i * TILE, (i + 1) * TILE)
        folded = jnp.zeros((TILE, LANES), F32)
        for j in range(COLS // TILE):
            cols = slice(j * TILE, (j + 1) * TILE)
            scores = scores_ref[rows, cols] + band_scores(ordered_ref, 3, far_ref, rows, cols)
            live = live_ref[i, j][:1, :1] > 0.0
            part = jnp.where(live, jnp.exp(scores * SHARPNESS), 0.0)
            kernel_ref[rows, cols] = part
            for k in range(TILE // LANES):
                folded = folded + part[:, k * LANES : (k + 1) * LANES]
        folded_ref[rows, :] = folded
    own = mass_ref[...]
    sums = jnp.concatenate([lane_sums(folded_ref[...]), own, own], axis=0)
    sums_ref[...] = jnp.broadcast_to(sums[None], sums_ref.shape)


def first_columns_body(kernel_ref, parts_ref, mass_ref, out_ref):
    half = CHUNKS // 2
    mass = jnp.concatenate([parts_ref[k, CHUNKS : CHUNKS + half, :] for k in range(2)], axis=0)
    mass_ref[...] = mass
    column_sums(kernel_ref, mass / jnp.sum(parts_ref[:, :CHUNKS, :], axis=0), out_ref)


def columns_body(kernel_ref, mass_ref, *refs):
    part_refs, out_ref = refs[:4], refs[4]
    total = sum(part[...] for part in part_refs)
    column_sums(kernel_ref, mass_ref[...] / total, out_ref)


def last_columns_body(kernel_ref, mass_ref, side_ref, *refs):
    part_refs, (log_ref, out_ref) = refs[:4], refs[4:]
    scale = mass_ref[...] / sum(part[...] for part in part_refs)
    log_ref[...] = jnp.log(
        jnp.where(side_ref[...] == 0.0, scale[: CHUNKS // 2], scale[CHUNKS // 2 :])
    )
    column_sums(kernel_ref, scale, out_ref)


def column_sums(kernel_ref, scale, out_ref):
    acc = [None] * (COLS // LANES)
    for i in range(CHUNKS):
        wide = jnp.broadcast_to(scale[i : i + 1, :], (LANES, LANES)).T
        for j in range(COLS // LANES):
            prod = kernel_ref[i * LANES : (i + 1) * LANES, j * LANES : (j + 1) * LANES] * wide
            prod = jnp.sum(prod.reshape(LANES // 8, 8, LANES), axis=0)
            acc[j] = prod if acc[j] is None else acc[j] + prod
    sums = jnp.concatenate([jnp.sum(a, axis=0, keepdims=True) for a in acc], axis=0)
    out_ref[...] = jnp.broadcast_to(sums[None], out_ref.shape)


def rows_body(kernel_ref, mass_ref, parts_ref, sums_ref, folded_ref):
    scale = mass_ref[...] / jnp.sum(parts_ref[...], axis=0)
    for i in range(CHUNKS):
        rows = slice(i * LANES, (i + 1) * LANES)
        total = kernel_ref[rows, :LANES] * scale[0:1, :]
        for j in range(1, COLS // LANES):
            total = total + kernel_ref[rows, j * LANES : (j + 1) * LANES] * scale[j : j + 1, :]
        folded_ref[rows, :] = total
    sums_ref[...] = lane_sums(folded_ref[...])


HALF = jax.ShapeDtypeStruct((CHUNKS // 2, LANES), F32)
SMALL = jax.ShapeDtypeStruct((CHUNKS, LANES), F32)
WIDE = pltpu.VMEM((N_Z * N_Y, CHUNKS, LANES), F32)
RING = (2 * N_X, CHUNKS, LANES)
KERNEL = pltpu.VMEM((ROWS, COLS), F32)
HALF_BAND = pltpu.VMEM((N_Z * GROUP, COLS), jnp.bfloat16)
BUILD = pltpu.CompilerParams(vmem_limit_bytes=28 * 1024 * 1024)
SWEEP = pltpu.CompilerParams(vmem_limit_bytes=16 * 1024 * 1024)


def work(bands):
    return pl.CostEstimate(
        flops=2 * ROWS * COLS * BAND * bands, bytes_accessed=8_000_000, transcendentals=0
    )


def shards(src_emb, tgt_emb, tile_mask, src_mass, tgt_mass):
    src = src_emb[0]
    src_a = [wheel_x(src, 1), wheel_x(src, -1), wheel_x(src, 2)]
    sent = pl.pallas_call(
        halves_body,
        out_shape=jax.ShapeDtypeStruct((2 * N_Z, GROUP, COLS), jnp.bfloat16),
        in_specs=[VMEM],
        out_specs=VMEM,
        compiler_params=SWEEP,
    )(tgt_emb[0])
    own_band = lax.all_to_all(sent, ("z", "xl"), 0, 0, tiled=True).reshape(BAND, COLS)
    split_band = pl.pallas_call(
        split_body,
        out_shape=(HALF_BAND, HALF_BAND),
        in_specs=[VMEM],
        out_specs=(VMEM, VMEM),
        compiler_params=SWEEP,
    )(own_band)
    swapped = [shift(s, "c", 2, 1) for s in (src, src_a[0])]
    near = [wheel_y(v, 1) for v in split_band]
    away = wheel_y(own_band, -1)
    *late, _ = lax.optimization_barrier((src_a[1], src_a[2], near[1]))
    swapped += [shift(s, "c", 2, 1) for s in late]
    far = [wheel_y(v, 1) for v in near]

    where = jnp.stack([lax.axis_index(a) for a in ("y", "c", "xh", "xl")]).astype(jnp.int32)
    scores, ordered, live, tgt_cols, side = pl.pallas_call(
        prepare_body,
        out_shape=(
            KERNEL,
            pltpu.VMEM((VECTOR_DIMENSION, ROWS), jnp.bfloat16),
            pltpu.VMEM((ROWS // TILE, COLS // TILE, 8, LANES), F32),
            SMALL,
            HALF,
        ),
        in_specs=[SMEM] + [HBM] * 3 + [VMEM] * 8,
        out_specs=(VMEM,) * 5,
        scratch_shapes=[
            pltpu.VMEM((VECTOR_DIMENSION, ROWS), jnp.bfloat16),
            pltpu.SMEM(tile_mask.shape, jnp.int32),
            pltpu.VMEM((2 * CHUNKS, LANES), F32),
            pltpu.SemaphoreType.DMA((3,)),
        ],
        compiler_params=BUILD,
        cost_estimate=work(1),
    )(where, *map(in_hbm, (tile_mask, tgt_mass.reshape(-1, LANES), src)), *src_a, *swapped, own_band)
    ordered = in_vmem(ordered)
    scores = pl.pallas_call(
        partial_body,
        out_shape=KERNEL,
        in_specs=[VMEM] * 5,
        out_specs=VMEM,
        scratch_shapes=[pltpu.VMEM((BAND, COLS), jnp.bfloat16)],
        compiler_params=BUILD,
        cost_estimate=work(2),
    )(ordered, in_vmem(scores), *near, away)
    own = src_mass.reshape(-1, LANES)
    kernel, sums = pl.pallas_call(
        build_body,
        out_shape=(KERNEL, pltpu.VMEM((2 * N_X, 2 * CHUNKS, LANES), F32)),
        in_specs=[VMEM] * 6,
        out_specs=(VMEM, VMEM),
        scratch_shapes=[pltpu.VMEM((ROWS, LANES), F32), pltpu.VMEM((BAND, COLS), jnp.bfloat16)],
        compiler_params=BUILD,
        cost_estimate=work(1),
    )(ordered, in_vmem(scores), in_vmem(live), own, *far)

    kernel = in_vmem(kernel)
    for sweep in range(ITERS):
        if sweep == 0:
            parts = [lax.all_to_all(sums, ("xh", "c", "xl"), 0, 0, tiled=True)]
        else:
            parts = ring_parts(sums)
        if sweep == 0:
            body, operands, extra = first_columns_body, (), (SMALL,)
        elif sweep < ITERS - 1:
            body, operands, extra = columns_body, (mass,), ()
        else:
            body, operands, extra = last_columns_body, (mass, side), (HALF,)
        outs = pl.pallas_call(
            body,
            out_shape=(*extra, WIDE),
            in_specs=[VMEM] * (1 + len(operands) + len(parts)),
            out_specs=(VMEM,) * (1 + len(extra)),
            compiler_params=SWEEP,
        )(kernel, *operands, *parts)
        if sweep == 0:
            mass = outs[0]
        parts = lax.all_to_all(outs[-1], PLANE, 0, 0, tiled=True)
        if sweep < ITERS - 1:
            sums = pl.pallas_call(
                rows_body,
                out_shape=SMALL,
                in_specs=[VMEM] * 3,
                out_specs=VMEM,
                scratch_shapes=[pltpu.VMEM((ROWS, LANES), F32)],
                compiler_params=SWEEP,
            )(kernel, tgt_cols, parts)

    log_src = outs[0]
    mine = jnp.log(tgt_cols / jnp.sum(parts, axis=0)).reshape(-1)
    theirs = shift(mine, "xl", 2, 1)
    log_tgt = jnp.where(lax.axis_index("xl") == 0, jnp.concatenate([mine, theirs]), jnp.concatenate([theirs, mine]))
    return log_src.reshape(-1), log_tgt


def solution(mesh):
    fine = Mesh(mesh.devices.reshape(N_Z, N_Y, 2, 2, 2), ("z", "y", "xh", "c", "xl"))
    placed = (
        P("xl", ("xh", "c"), ("z", "y")),
        P("xl", ("z", "y"), ("xh", "c")),
        P(("z", "y"), ("xh", "c")),
        P(("z", "y", "xl")),
        P(("xh", "c")),
    )
    return jax.shard_map(
        shards,
        mesh=fine,
        in_specs=placed,
        out_specs=(P(("z", "y", "xl")), P(("xh", "c"))),
        check_vma=False,
    )
```

```python
import math

import jax
import jax.numpy as jnp
from jax import lax
from jax.experimental import pallas as pl
from jax.experimental.pallas import tpu as pltpu
from jax.sharding import Mesh
from jax.sharding import PartitionSpec as P

VECTOR_DIMENSION = 1024
TILE = 512
ITERS = 3
SHARPNESS = 1.0 / (0.64 * math.sqrt(VECTOR_DIMENSION))

X = ("xh", "xl")
PLANE = ("z", "y")
N_Z, N_Y, N_X = 8, 4, 4
ROWS = 1024
COLS = 1024
LANES = 128
CHUNKS = ROWS // LANES
GROUP = 16
F32 = jnp.float32
VMEM = pl.BlockSpec(memory_space=pltpu.VMEM)
HBM = pl.BlockSpec(memory_space=pltpu.HBM)
SMEM = pl.BlockSpec(memory_space=pltpu.SMEM)


def shift(value, axis, size, by):
    return lax.ppermute(value, axis, [(i, (i + by) % size) for i in range(size)])


def wheel_y(value, by):
    pairs = [
        (i * 2 + c, (i + (by if c == 0 else -by)) % N_Y * 2 + c) for i in range(N_Y) for c in range(2)
    ]
    return lax.ppermute(value, ("y", "c"), pairs)


def wheel_x(value, by):
    place = lambda x, c: x // 2 * 4 + c * 2 + x % 2
    pairs = [
        (place(i, c), place((i + (by if c == 0 else -by)) % N_X, c)) for i in range(N_X) for c in range(2)
    ]
    return lax.ppermute(value, ("xh", "c", "xl"), pairs)


def ring_parts(sums):
    chip = sums + shift(sums, "c", 2, 1)
    one, far = wheel_x(chip, 1), shift(chip, X, N_X, 2)
    return [chip, one, far, shift(one, "c", 2, 1)]


def in_vmem(value):
    return pltpu.with_memory_space_constraint(value, pltpu.VMEM)


def in_hbm(value):
    return pltpu.with_memory_space_constraint(value, pltpu.HBM)


def lane_sums(folded):
    parts = [
        jnp.sum(folded[i * LANES : (i + 1) * LANES, :].T, axis=0, keepdims=True)
        for i in range(folded.shape[0] // LANES)
    ]
    return jnp.concatenate(parts, axis=0)


def turned(value, size):
    return lax.rem(value + size, size)


CONTRACT = (((0,), (0,)), ((), ()))
TURNS = (0, -1, 1, 2)
BAND = 2 * N_Z * GROUP


def halves_body(tgt_ref, out_ref):
    for z in range(N_Z):
        for low in range(2):
            out_ref[z * 2 + low] = tgt_ref[:, low * COLS : (low + 1) * COLS]


def prepare_body(where_ref, mask_hbm, tgt_mass_hbm, src_hbm, *refs):
    src_refs, block_ref = refs[:7], refs[7]
    scores_ref, ordered_ref, live_ref, tgt_cols_ref, side_ref = refs[8:13]
    src_ref, mask_ref, tgt_mass_ref, sems = refs[13:]
    y, c, xh, xl = (where_ref[i] for i in range(4))

    def src_at(core, turn):
        x = turned(xh * 2 + xl + turn * (1 - 2 * core), N_X)
        to = lax.rem(x, 2) * 512 + lax.div(x, 2) * 256 + core * 128
        return src_ref.at[pl.ds(pl.multiple_of(to, LANES), LANES), :]

    fetches = [
        pltpu.make_async_copy(src_hbm, src_at(c, 0), sems.at[0]),
        pltpu.make_async_copy(mask_hbm, mask_ref, sems.at[1]),
        pltpu.make_async_copy(tgt_mass_hbm, tgt_mass_ref, sems.at[2]),
    ]
    for fetch in fetches:
        fetch.start()
    for index, part in enumerate(src_refs):
        core, turn = (c, index + 1) if index < 3 else (1 - c, index - 3)
        src_at(core, TURNS[turn])[...] = part[...]
    for fetch in fetches:
        fetch.wait()
    for band, turn in enumerate(TURNS):
        at_y = turned(y + turn * (1 - 2 * c), N_Y)
        for z in range(N_Z):
            for low in range(2):
                to = band * BAND + (z * 2 + low) * GROUP
                at = pl.multiple_of(low * 512 + z * (N_Y * GROUP) + at_y * GROUP, GROUP)
                ordered_ref[to : to + GROUP, :] = src_ref[pl.ds(at, GROUP), :]
    tgt_cols_ref[...] = jnp.where(xl == 0, tgt_mass_ref[:CHUNKS, :], tgt_mass_ref[CHUNKS:, :])
    side_ref[...] = jnp.full(side_ref.shape, xl.astype(F32))
    for i in range(ROWS // TILE):
        rows = slice(i * TILE, (i + 1) * TILE)
        for j in range(COLS // TILE):
            cols = slice(j * TILE, (j + 1) * TILE)
            live = mask_ref[i, xl * (COLS // TILE) + j] > 0
            live_ref[i, j] = jnp.full((8, LANES), live.astype(F32))
            scores_ref[rows, cols] = band_scores(ordered_ref, 0, block_ref, rows, cols)


def band_scores(ordered_ref, band, block_ref, rows, cols):
    return lax.dot_general(
        ordered_ref[band * BAND : (band + 1) * BAND, rows],
        block_ref[:, cols],
        CONTRACT,
        preferred_element_type=F32,
    )


def split_body(band_ref, first_ref, second_ref):
    first_ref[...] = band_ref[: BAND // 2, :]
    second_ref[...] = band_ref[BAND // 2 :, :]


def joined(ref, halves):
    for k, half in enumerate(halves):
        ref[k * BAND // 2 : (k + 1) * BAND // 2, :] = half[...]


def partial_body(ordered_ref, scores_ref, near_0_ref, near_1_ref, away_ref, out_ref, near_ref):
    joined(near_ref, (near_0_ref, near_1_ref))
    for i in range(ROWS // TILE):
        rows = slice(i * TILE, (i + 1) * TILE)
        for j in range(COLS // TILE):
            cols = slice(j * TILE, (j + 1) * TILE)
            out_ref[rows, cols] = (
                scores_ref[rows, cols]
                + band_scores(ordered_ref, 1, near_ref, rows, cols)
                + band_scores(ordered_ref, 2, away_ref, rows, cols)
            )


def build_body(
    ordered_ref, scores_ref, live_ref, mass_ref, far_0_ref, far_1_ref, kernel_ref, sums_ref, folded_ref, far_ref
):
    joined(far_ref, (far_0_ref, far_1_ref))
    for i in range(ROWS // TILE):
        rows = slice(i * TILE, (i + 1) * TILE)
        folded = jnp.zeros((TILE, LANES), F32)
        for j in range(COLS // TILE):
            cols = slice(j * TILE, (j + 1) * TILE)
            scores = scores_ref[rows, cols] + band_scores(ordered_ref, 3, far_ref, rows, cols)
            live = live_ref[i, j][:1, :1] > 0.0
            part = jnp.where(live, jnp.exp(scores * SHARPNESS), 0.0)
            kernel_ref[rows, cols] = part
            for k in range(TILE // LANES):
                folded = folded + part[:, k * LANES : (k + 1) * LANES]
        folded_ref[rows, :] = folded
    own = mass_ref[...]
    sums_ref[...] = jnp.concatenate([lane_sums(folded_ref[...]), own, own], axis=0)


def first_columns_body(kernel_ref, side_ref, *refs):
    part_refs, (mass_ref, out_ref) = refs[:4], refs[4:]
    half = CHUNKS // 2
    own, other = (part_refs[k][CHUNKS : CHUNKS + half, :] * 0.5 for k in range(2))
    first = side_ref[...] == 0.0
    mass = jnp.concatenate([jnp.where(first, own, other), jnp.where(first, other, own)], axis=0)
    mass_ref[...] = mass
    column_sums(kernel_ref, mass / sum(part[:CHUNKS, :] for part in part_refs), out_ref)


def columns_body(kernel_ref, mass_ref, *refs):
    part_refs, out_ref = refs[:4], refs[4]
    total = sum(part[...] for part in part_refs)
    column_sums(kernel_ref, mass_ref[...] / total, out_ref)


def last_columns_body(kernel_ref, mass_ref, side_ref, *refs):
    part_refs, (log_ref, out_ref) = refs[:4], refs[4:]
    scale = mass_ref[...] / sum(part[...] for part in part_refs)
    log_ref[...] = jnp.log(
        jnp.where(side_ref[...] == 0.0, scale[: CHUNKS // 2], scale[CHUNKS // 2 :])
    )
    column_sums(kernel_ref, scale, out_ref)


def column_sums(kernel_ref, scale, out_ref):
    acc = [None] * (COLS // LANES)
    for i in range(CHUNKS):
        wide = jnp.broadcast_to(scale[i : i + 1, :], (LANES, LANES)).T
        for j in range(COLS // LANES):
            prod = kernel_ref[i * LANES : (i + 1) * LANES, j * LANES : (j + 1) * LANES] * wide
            prod = jnp.sum(prod.reshape(LANES // 8, 8, LANES), axis=0)
            acc[j] = prod if acc[j] is None else acc[j] + prod
    sums = jnp.concatenate([jnp.sum(a, axis=0, keepdims=True) for a in acc], axis=0)
    out_ref[...] = jnp.broadcast_to(sums[None], out_ref.shape)


def rows_body(kernel_ref, mass_ref, parts_ref, sums_ref, folded_ref):
    scale = mass_ref[...] / jnp.sum(parts_ref[...], axis=0)
    for i in range(CHUNKS):
        rows = slice(i * LANES, (i + 1) * LANES)
        total = kernel_ref[rows, :LANES] * scale[0:1, :]
        for j in range(1, COLS // LANES):
            total = total + kernel_ref[rows, j * LANES : (j + 1) * LANES] * scale[j : j + 1, :]
        folded_ref[rows, :] = total
    sums_ref[...] = lane_sums(folded_ref[...])


HALF = jax.ShapeDtypeStruct((CHUNKS // 2, LANES), F32)
SMALL = jax.ShapeDtypeStruct((CHUNKS, LANES), F32)
WIDE = pltpu.VMEM((N_Z * N_Y, CHUNKS, LANES), F32)
RING = (2 * N_X, CHUNKS, LANES)
KERNEL = pltpu.VMEM((ROWS, COLS), F32)
HALF_BAND = pltpu.VMEM((N_Z * GROUP, COLS), jnp.bfloat16)
BUILD = pltpu.CompilerParams(vmem_limit_bytes=28 * 1024 * 1024)
SWEEP = pltpu.CompilerParams(vmem_limit_bytes=16 * 1024 * 1024)


def work(bands):
    return pl.CostEstimate(
        flops=2 * ROWS * COLS * BAND * bands, bytes_accessed=8_000_000, transcendentals=0
    )


def shards(src_emb, tgt_emb, tile_mask, src_mass, tgt_mass):
    src = src_emb[0]
    src_a = [wheel_x(src, 1), wheel_x(src, -1), wheel_x(src, 2)]
    sent = pl.pallas_call(
        halves_body,
        out_shape=jax.ShapeDtypeStruct((2 * N_Z, GROUP, COLS), jnp.bfloat16),
        in_specs=[VMEM],
        out_specs=VMEM,
        compiler_params=SWEEP,
    )(tgt_emb[0])
    own_band = lax.all_to_all(sent, ("z", "xl"), 0, 0, tiled=True).reshape(BAND, COLS)
    split_band = pl.pallas_call(
        split_body,
        out_shape=(HALF_BAND, HALF_BAND),
        in_specs=[VMEM],
        out_specs=(VMEM, VMEM),
        compiler_params=SWEEP,
    )(own_band)
    swapped = [shift(s, "c", 2, 1) for s in (src, *src_a[:2])]
    near = [wheel_y(v, 1) for v in split_band]
    away = wheel_y(own_band, -1)
    late, _ = lax.optimization_barrier((src_a[2], near[0]))
    swapped.append(shift(late, "c", 2, 1))
    far = [wheel_y(v, 1) for v in near]

    where = jnp.stack([lax.axis_index(a) for a in ("y", "c", "xh", "xl")]).astype(jnp.int32)
    scores, ordered, live, tgt_cols, side = pl.pallas_call(
        prepare_body,
        out_shape=(
            KERNEL,
            pltpu.VMEM((VECTOR_DIMENSION, ROWS), jnp.bfloat16),
            pltpu.VMEM((ROWS // TILE, COLS // TILE, 8, LANES), F32),
            SMALL,
            HALF,
        ),
        in_specs=[SMEM] + [HBM] * 3 + [VMEM] * 8,
        out_specs=(VMEM,) * 5,
        scratch_shapes=[
            pltpu.VMEM((VECTOR_DIMENSION, ROWS), jnp.bfloat16),
            pltpu.SMEM(tile_mask.shape, jnp.int32),
            pltpu.VMEM((2 * CHUNKS, LANES), F32),
            pltpu.SemaphoreType.DMA((3,)),
        ],
        compiler_params=BUILD,
        cost_estimate=work(1),
    )(where, *map(in_hbm, (tile_mask, tgt_mass.reshape(-1, LANES), src)), *src_a, *swapped, own_band)
    ordered = in_vmem(ordered)
    scores = pl.pallas_call(
        partial_body,
        out_shape=KERNEL,
        in_specs=[VMEM] * 5,
        out_specs=VMEM,
        scratch_shapes=[pltpu.VMEM((BAND, COLS), jnp.bfloat16)],
        compiler_params=BUILD,
        cost_estimate=work(2),
    )(ordered, in_vmem(scores), *near, away)
    own = src_mass.reshape(-1, LANES)
    kernel, sums = pl.pallas_call(
        build_body,
        out_shape=(KERNEL, jax.ShapeDtypeStruct((2 * CHUNKS, LANES), F32)),
        in_specs=[VMEM] * 6,
        out_specs=(VMEM, VMEM),
        scratch_shapes=[pltpu.VMEM((ROWS, LANES), F32), pltpu.VMEM((BAND, COLS), jnp.bfloat16)],
        compiler_params=BUILD,
        cost_estimate=work(1),
    )(ordered, in_vmem(scores), in_vmem(live), own, *far)

    kernel = in_vmem(kernel)
    for sweep in range(ITERS):
        parts = ring_parts(sums)
        if sweep == 0:
            body, operands, extra = first_columns_body, (side,), (SMALL,)
        elif sweep < ITERS - 1:
            body, operands, extra = columns_body, (mass,), ()
        else:
            body, operands, extra = last_columns_body, (mass, side), (HALF,)
        outs = pl.pallas_call(
            body,
            out_shape=(*extra, WIDE),
            in_specs=[VMEM] * (1 + len(operands) + len(parts)),
            out_specs=(VMEM,) * (1 + len(extra)),
            compiler_params=SWEEP,
        )(kernel, *operands, *parts)
        if sweep == 0:
            mass = outs[0]
        parts = lax.all_to_all(outs[-1], PLANE, 0, 0, tiled=True)
        if sweep < ITERS - 1:
            sums = pl.pallas_call(
                rows_body,
                out_shape=SMALL,
                in_specs=[VMEM] * 3,
                out_specs=VMEM,
                scratch_shapes=[pltpu.VMEM((ROWS, LANES), F32)],
                compiler_params=SWEEP,
            )(kernel, tgt_cols, parts)

    log_src = outs[0]
    mine = jnp.log(tgt_cols / jnp.sum(parts, axis=0)).reshape(-1)
    theirs = shift(mine, "xl", 2, 1)
    log_tgt = jnp.where(lax.axis_index("xl") == 0, jnp.concatenate([mine, theirs]), jnp.concatenate([theirs, mine]))
    return log_src.reshape(-1), log_tgt


def solution(mesh):
    fine = Mesh(mesh.devices.reshape(N_Z, N_Y, 2, 2, 2), ("z", "y", "xh", "c", "xl"))
    placed = (
        P("xl", ("xh", "c"), ("z", "y")),
        P("xl", ("z", "y"), ("xh", "c")),
        P(("z", "y"), ("xh", "c")),
        P(("z", "y", "xl")),
        P(("xh", "c")),
    )
    return jax.shard_map(
        shards,
        mesh=fine,
        in_specs=placed,
        out_specs=(P(("z", "y", "xl")), P(("xh", "c"))),
        check_vma=False,
    )
```
